128 devices in a mesh: ctx: 128 (over y, z, x, core).
Axes of the slice: x: 4, y: 4, z: 4, core: 2. Of those that a mesh axis runs over, the one named last changes fastest.
Arguments:
- query_rows: bfloat16 [32768, 32, 128], P('ctx'), may hold values from -6 to 6
- key_rows: bfloat16 [32768, 16, 128], P('ctx'), may hold values from -6 to 6
- value_rows: bfloat16 [32768, 16, 128], P('ctx'), may hold values from -6 to 6
- grad_out: bfloat16 [4096, 32768], P('ctx'), may hold values from -6 to 6
Outputs:
- grad_query: bfloat16 [32768, 32, 128], P('ctx')
- grad_key: bfloat16 [32768, 16, 128], P('ctx')
- grad_value: bfloat16 [32768, 16, 128], P('ctx')
The draws below stay inside these ranges and needn't reach their ends.
All inputs are finite; a program needn't handle non-finite values.
Results may differ from the reference program's by a relative error of at most 0.019.
Values may be sent and summed in bfloat16 or wider, within the bound.
A program may use at most 128 MiB of HBM per device.

```python
import jax
import jax.numpy as jnp
from jax import lax

H = 32
KVH = 16
DH = 128
W = 1024
TOK_DEV = 256
SEQ = 32768


def draw_query_rows(key, part):
    values = jnp.clip(jax.random.normal(jax.random.fold_in(key, 1), (SEQ, H, DH), jnp.float32), -4.0, 4.0)
    return values.astype(jnp.bfloat16)


def draw_key_rows(key, part):
    values = jnp.clip(jax.random.normal(jax.random.fold_in(key, 2), (SEQ, KVH, DH), jnp.float32), -4.0, 4.0)
    return values.astype(jnp.bfloat16)


def levels(own_key, dims, pieces, least, top_value):
    factor_of = 1.0
    for axis_at, blocks in pieces:
        steps = jax.random.uniform(jax.random.fold_in(jax.random.fold_in(own_key, 6), axis_at), (blocks,), jnp.float32, least / len(pieces), top_value / len(pieces))
        factor_of = factor_of * jnp.repeat(jnp.exp(steps), dims[axis_at] // blocks).reshape((-1,) + (1,) * (len(dims) - 1 - axis_at))
    return factor_of


def scatter_about(own_key, dims, scale, reach, pieces=(), kind=jnp.bfloat16):
    result = jax.random.normal(own_key, dims, jnp.float32) * scale
    if len(pieces) > 0:
        result = levels(own_key, dims, pieces, -0.22, 0.18) * result
    return jnp.clip(result, min=-reach, max=reach).astype(kind)


def setup_inputs(seed: int = 0) -> dict:
    arg_keys = jax.random.split(jax.random.key(seed), 5)
    return {
        "query_rows": draw_query_rows(jax.random.fold_in(arg_keys[4], 71), 0),
        "key_rows": draw_key_rows(jax.random.fold_in(arg_keys[4], 71), 0),
        "value_rows": scatter_about(arg_keys[2], (SEQ, KVH, DH), 1.0, 6.0, ((0, 128),)),
        "grad_out": scatter_about(arg_keys[3], (H * DH, SEQ), 1.0, 6.0, ((0, 128),)),
    }


query_scale = 1.0 / 12.0


def reference(query_rows, key_rows, value_rows, grad_out):
    blocks = SEQ // TOK_DEV
    key_pad = jnp.concatenate([jnp.zeros((W, KVH, DH), jnp.bfloat16), key_rows], axis=0)
    value_pad = jnp.concatenate([jnp.zeros((W, KVH, DH), jnp.bfloat16), value_rows], axis=0)
    row_pos = jnp.arange(TOK_DEV, dtype=jnp.int32)[:, None]
    col_pos = jnp.arange(W + TOK_DEV, dtype=jnp.int32)[None, :]

    def step(carry, index):
        acc_key, acc_value = carry
        start = (index * TOK_DEV).astype(jnp.int32)
        q_block = lax.dynamic_slice_in_dim(query_rows, start, TOK_DEV, 0).reshape(TOK_DEV, KVH, 2, DH).astype(jnp.float32)
        k_window = lax.dynamic_slice_in_dim(key_pad, start, W + TOK_DEV, 0).astype(jnp.float32)
        v_window = lax.dynamic_slice_in_dim(value_pad, start, W + TOK_DEV, 0).astype(jnp.float32)
        do_block = lax.dynamic_slice_in_dim(grad_out, start, TOK_DEV, 1).reshape(KVH, 2, DH, TOK_DEV).astype(jnp.float32)
        allowed = (col_pos > row_pos) & (col_pos <= row_pos + W) & (start - W + col_pos >= 0)
        scores = jnp.einsum("tghd,kgd->ghtk", q_block, k_window) * query_scale
        masked = jnp.where(allowed, scores, -1e30)
        top = jnp.max(masked, axis=-1, keepdims=True)
        weights = jnp.exp(masked - top)
        probs = (weights / jnp.sum(weights, axis=-1, keepdims=True)).astype(jnp.bfloat16).astype(jnp.float32)
        dprobs = jnp.einsum("ghdt,kgd->ghtk", do_block, v_window)
        delta = jnp.sum(probs * dprobs, axis=-1, keepdims=True)
        dscores = (probs * (dprobs - delta) * query_scale).astype(jnp.bfloat16).astype(jnp.float32)
        dq_block = jnp.einsum("ghtk,kgd->tghd", dscores, k_window).astype(jnp.bfloat16)
        dv_part = jnp.einsum("ghtk,ghdt->kgd", probs, do_block).astype(jnp.bfloat16)
        dk_part = jnp.einsum("ghtk,tghd->kgd", dscores, q_block).astype(jnp.bfloat16)
        old_key = lax.dynamic_slice_in_dim(acc_key, start, W + TOK_DEV, 0)
        old_value = lax.dynamic_slice_in_dim(acc_value, start, W + TOK_DEV, 0)
        acc_key = lax.dynamic_update_slice_in_dim(acc_key, old_key + dk_part.astype(jnp.float32), start, 0)
        acc_value = lax.dynamic_update_slice_in_dim(acc_value, old_value + dv_part.astype(jnp.float32), start, 0)
        return (acc_key, acc_value), dq_block

    init = (jnp.zeros((SEQ + W, KVH, DH), jnp.float32), jnp.zeros((SEQ + W, KVH, DH), jnp.float32))
    (acc_key, acc_value), dq_all = lax.scan(step, init, jnp.arange(blocks, dtype=jnp.int32))
    grad_query = dq_all.reshape(SEQ, H, DH)
    return grad_query, acc_key[W:].astype(jnp.bfloat16), acc_value[W:].astype(jnp.bfloat16)
```

```python
import functools

import jax
import jax.numpy as jnp
from jax import lax
from jax.experimental import pallas as pl
from jax.experimental.pallas import tpu as pltpu
from jax.sharding import PartitionSpec as P

MESH = pl.DeviceIdType.MESH
SCALE = 1.0 / 12.0
LOG2E = 1.4426950408889634
T = 256
D = 128
HK = 8
NEG = -1e30

NT = (((1,), (1,)), ((), ()))
TN = (((0,), (0,)), ((), ()))


def dot(a, b, dims=(((1,), (0,)), ((), ()))):
    return lax.dot_general(a, b, dims, preferred_element_type=jnp.float32)


def attend(i, first, kv, q, do, s_scr, p_scr, g_scr, ds_scr, acc, dq):
    row = lax.broadcasted_iota(jnp.int32, (T, T), 0)
    col = lax.broadcasted_iota(jnp.int32, (T, T), 1)
    after = row > col
    after = jnp.concatenate([after, after], axis=1)
    for b in range(2):
        qb = q[b, pl.ds(2 * i, 2)].reshape(2 * T, D)
        dob = jnp.concatenate(
            [do[2 * i, :, b * T : (b + 1) * T], do[2 * i + 1, :, b * T : (b + 1) * T]], axis=1
        )
        tops = []
        for j in range(5):
            rows = pl.ds((b + j) * T, T)
            s = dot(kv[i, 0, rows, :], qb, NT)
            if j == 0:
                s = jnp.where(after, s, NEG)
            if j == 4:
                s = jnp.where(after, NEG, s)
            s_scr[pl.ds(j * T, T), :] = s
            t = jnp.max(s, axis=0, keepdims=True)
            if j < 4:
                t = jnp.where(first + b + j >= 0, t, NEG)
            tops.append(t)
        top = functools.reduce(jnp.maximum, tops)
        total = jnp.zeros((1, 2 * T), jnp.float32)
        delta = jnp.zeros((1, 2 * T), jnp.float32)
        for j in range(5):
            rows = pl.ds((b + j) * T, T)
            here = pl.ds(j * T, T)
            t = top
            if j < 4:
                t = jnp.where(first + b + j >= 0, top, -NEG)
            p = jnp.exp2((s_scr[here, :] - t) * (SCALE * LOG2E))
            g = dot(kv[i, 1, rows, :], dob)
            total = total + jnp.sum(p, axis=0, keepdims=True)
            delta = delta + jnp.sum(p * g, axis=0, keepdims=True)
            p_scr[here, :] = p
            g_scr[here, :] = g
        inv = 1.0 / total
        delta = delta * inv
        for j in range(5):
            rows = pl.ds((b + j) * T, T)
            here = pl.ds(j * T, T)
            p = p_scr[here, :] * inv
            ds = (p * (g_scr[here, :] - delta)).astype(jnp.bfloat16)
            ds_scr[here, :] = ds
            dv = dot(p.astype(jnp.bfloat16), dob, NT)
            dk = dot(ds, qb) * SCALE
            if b == 0 or j == 4:
                acc[i, 0, rows, :] = dk
                acc[i, 1, rows, :] = dv
            else:
                acc[i, 0, rows, :] += dk
                acc[i, 1, rows, :] += dv
        dqt = dot(kv[i, 0, pl.ds(b * T, 5 * T), :], ds_scr[...], TN)
        dq[b, pl.ds(2 * i, 2)] = (
            (jnp.transpose(dqt) * SCALE).astype(jnp.bfloat16).reshape(2, T, D)
        )


def kernel(
    n, q_in, k_in, v_in, do_in, dq_out, dkv_out,
    kv, q, do, dq, s_scr, p_scr, g_scr, ds_scr, acc,
    part_a, got_a, part_b, got_b, fin,
    loc_sem, d2d_send, d2d_recv, fb_send, fb_recv, fa_send, fa_recv,
    ra_send, ra_recv, rb_send, rb_recv, out_loc, out_send, out_recv,
):
    me = lax.axis_index("ctx")
    core = lax.rem(me, 2)
    chip = me // 2
    sib = 2 * chip + (1 - core)
    nxt = lax.rem(me + 2, n)
    prv = lax.rem(me + n - 2, n)

    barrier = pltpu.get_barrier_semaphore()
    for other in (sib, nxt, prv):
        pl.semaphore_signal(barrier, inc=1, device_id=(other,), device_id_type=MESH)
    pl.semaphore_wait(barrier, 3)

    def remote(src, dst, send, recv, dev):
        return pltpu.make_async_remote_copy(
            src_ref=src, dst_ref=dst, send_sem=send, recv_sem=recv,
            device_id=(dev,), device_id_type=MESH,
        )

    slab = pl.ds(pl.multiple_of(core * T, T), T)
    own = pl.ds(pl.multiple_of(4 * T + core * T, T), T)
    mine8 = pl.ds(HK * core, HK)
    theirs8 = pl.ds(HK * (1 - core), HK)
    mine16 = pl.ds(2 * HK * core, 2 * HK)
    theirs16 = pl.ds(2 * HK * (1 - core), 2 * HK)

    starts = [
        (k_in, mine8, theirs8, kv.at[:, 0, own]),
        (v_in, mine8, theirs8, kv.at[:, 1, own]),
        (q_in, mine16, theirs16, q.at[core]),
        (do_in, mine16, theirs16, do.at[:, :, slab]),
    ]
    local, cross = [], []
    for at, (src, mine, theirs, dst) in enumerate(starts):
        cross.append(remote(src.at[theirs], dst, d2d_send.at[at], d2d_recv.at[at], sib))
        local.append(pltpu.make_async_copy(src.at[mine], dst, loc_sem.at[at]))
        cross[-1].start()
        local[-1].start()

    def to_b(i):
        return remote(
            kv.at[i, :, pl.ds(4 * T, 2 * T)], kv.at[i, :, pl.ds(2 * T, 2 * T)],
            fb_send.at[i], fb_recv.at[i], nxt,
        )

    def to_a(i):
        return remote(
            kv.at[i, :, pl.ds(2 * T, 2 * T)], kv.at[i, :, pl.ds(0, 2 * T)],
            fa_send.at[i], fa_recv.at[i], nxt,
        )

    def back_a(i):
        return remote(part_a.at[i], got_a.at[i], ra_send.at[i], ra_recv.at[i], prv)

    def back_b(i):
        return remote(part_b.at[i], got_b.at[i], rb_send.at[i], rb_recv.at[i], prv)

    def dq_copies(i):
        heads = pl.ds(2 * (HK * core + i), 2)
        return (
            pltpu.make_async_copy(dq.at[core, pl.ds(2 * i, 2)], dq_out.at[heads], out_loc.at[0, i]),
            remote(
                dq.at[1 - core, pl.ds(2 * i, 2)], dq_out.at[heads],
                out_send.at[0, i], out_recv.at[0, i], sib,
            ),
        )

    def dkv_copies(i):
        head = HK * core + i
        other = pl.ds(pl.multiple_of((1 - core) * T, T), T)
        return (
            pltpu.make_async_copy(fin.at[i, :, slab], dkv_out.at[head], out_loc.at[1, i]),
            remote(
                fin.at[i, :, other], dkv_out.at[head], out_send.at[1, i], out_recv.at[1, i], sib
            ),
        )

    for at in (0, 1):
        local[at].wait()
        cross[at].wait_recv()
    for i in range(3):
        to_b(i).start()
    for at in (2, 3):
        local[at].wait()
        cross[at].wait_recv()
    to_b(0).wait_recv()
    to_a(0).start()

    first = 2 * chip - 4

    def back1(i):
        back_a(i).wait_recv()
        part_b[i] = (acc[i, :, 2 * T : 4 * T, :] + got_a[i].astype(jnp.float32)).astype(jnp.bfloat16)
        back_b(i).start()

    def back2(i):
        back_b(i).wait_recv()
        fin[i] = (acc[i, :, 4 * T :, :] + got_b[i].astype(jnp.float32)).astype(jnp.bfloat16)
        for copy in dkv_copies(i):
            copy.start()

    def step(i, carry):
        @pl.when(i + 1 < HK)
        def _():
            to_b(i + 1).wait_recv()
            to_a(i + 1).start()

        @pl.when(i + 3 < HK)
        def _():
            to_b(i + 3).start()

        to_a(i).wait_recv()
        attend(i, first, kv, q, do, s_scr, p_scr, g_scr, ds_scr, acc, dq)
        part_a[i] = acc[i, :, : 2 * T, :].astype(jnp.bfloat16)
        back_a(i).start()
        for copy in dq_copies(i):
            copy.start()

        @pl.when(i >= 1)
        def _():
            back1(i - 1)

        @pl.when(i >= 2)
        def _():
            back2(i - 2)

        return carry

    lax.fori_loop(0, HK, step, 0)
    back1(HK - 1)
    back2(HK - 2)
    back2(HK - 1)

    for copy in cross:
        copy.wait_send()

    def finish(i, carry):
        to_b(i).wait_send()
        to_a(i).wait_send()
        back_a(i).wait_send()
        back_b(i).wait_send()
        for here, there in (dq_copies(i), dkv_copies(i)):
            here.wait()
            there.wait()
        return carry

    lax.fori_loop(0, HK, finish, 0)


def on_device(query_rows, key_rows, value_rows, grad_out):
    n = lax.axis_size("ctx")
    gathered = lax.all_to_all(grad_out, "ctx", split_axis=1, concat_axis=0, tiled=True)
    do_in = gathered.reshape(4 * HK, D, T)
    q_in = jnp.transpose(query_rows, (1, 0, 2))
    k_in = jnp.transpose(key_rows, (1, 0, 2))
    v_in = jnp.transpose(value_rows, (1, 0, 2))
    dma = pltpu.SemaphoreType.DMA
    bf16, f32 = jnp.bfloat16, jnp.float32
    any_spec = pl.BlockSpec(memory_space=pl.ANY)
    dq_heads, dkv = pl.pallas_call(
        functools.partial(kernel, n),
        out_shape=(
            jax.ShapeDtypeStruct((4 * HK, T, D), bf16),
            jax.ShapeDtypeStruct((2 * HK, 2, T, D), bf16),
        ),
        in_specs=[any_spec] * 4,
        out_specs=(any_spec, any_spec),
        scratch_shapes=[
            pltpu.VMEM((HK, 2, 6 * T, D), bf16),
            pltpu.VMEM((2, 2 * HK, T, D), bf16),
            pltpu.VMEM((2 * HK, D, 2 * T), bf16),
            pltpu.VMEM((2, 2 * HK, T, D), bf16),
            pltpu.VMEM((5 * T, 2 * T), f32),
            pltpu.VMEM((5 * T, 2 * T), f32),
            pltpu.VMEM((5 * T, 2 * T), f32),
            pltpu.VMEM((5 * T, 2 * T), bf16),
            pltpu.VMEM((HK, 2, 6 * T, D), f32),
            pltpu.VMEM((HK, 2, 2 * T, D), bf16),
            pltpu.VMEM((HK, 2, 2 * T, D), bf16),
            pltpu.VMEM((HK, 2, 2 * T, D), bf16),
            pltpu.VMEM((HK, 2, 2 * T, D), bf16),
            pltpu.VMEM((HK, 2, 2 * T, D), bf16),
            dma((4,)), dma((4,)), dma((4,)),
            dma((HK,)), dma((HK,)), dma((HK,)), dma((HK,)),
            dma((HK,)), dma((HK,)), dma((HK,)), dma((HK,)),
            dma((2, HK)), dma((2, HK)), dma((2, HK)),
        ],
        compiler_params=pltpu.CompilerParams(
            collective_id=0, has_side_effects=True, vmem_limit_bytes=58 * 2**20
        ),
        cost_estimate=pl.CostEstimate(
            flops=14_000_000_000, bytes_accessed=12 * 2**20, transcendentals=10_000_000
        ),
    )(q_in, k_in, v_in, do_in)
    grad_query = jnp.transpose(dq_heads, (1, 0, 2))
    grad_key = jnp.transpose(dkv[:, 0], (1, 0, 2))
    grad_value = jnp.transpose(dkv[:, 1], (1, 0, 2))
    return (grad_query, grad_key, grad_value)


def solution(mesh):
    in_specs = (P("ctx", None, None), P("ctx", None, None), P("ctx", None, None), P("ctx", None))
    out_specs = (P("ctx", None, None), P("ctx", None, None), P("ctx", None, None))
    return jax.shard_map(
        on_device, mesh=mesh, in_specs=in_specs, out_specs=out_specs, check_vma=False
    )
```

```python
import functools

import jax
import jax.numpy as jnp
from jax import lax
from jax.experimental import pallas as pl
from jax.experimental.pallas import tpu as pltpu
from jax.sharding import PartitionSpec as P

MESH = pl.DeviceIdType.MESH
SCALE = 1.0 / 12.0
LOG2E = 1.4426950408889634
T = 256
D = 128
HK = 8
NEG = -1e30

NT = (((1,), (1,)), ((), ()))
TN = (((0,), (0,)), ((), ()))


def dot(a, b, dims=(((1,), (0,)), ((), ()))):
    return lax.dot_general(a, b, dims, preferred_element_type=jnp.float32)


def attend(i, first, kv, q, do, s_scr, p_scr, g_scr, ds_scr, acc, dq):
    row = lax.broadcasted_iota(jnp.int32, (T, T), 0)
    col = lax.broadcasted_iota(jnp.int32, (T, T), 1)
    after = row > col
    after = jnp.concatenate([after, after], axis=1)
    for b in range(2):
        qb = q[b, pl.ds(2 * i, 2)].reshape(2 * T, D)
        dob = jnp.concatenate(
            [do[2 * i, :, b * T : (b + 1) * T], do[2 * i + 1, :, b * T : (b + 1) * T]], axis=1
        )
        tops = []
        for j in range(5):
            rows = pl.ds((b + j) * T, T)
            s = dot(kv[i, 0, rows, :], qb, NT)
            if j == 0:
                s = jnp.where(after, s, NEG)
            if j == 4:
                s = jnp.where(after, NEG, s)
            s_scr[pl.ds(j * T, T), :] = s
            t = jnp.max(s, axis=0, keepdims=True)
            if j < 4:
                t = jnp.where(first + b + j >= 0, t, NEG)
            tops.append(t)
        top = functools.reduce(jnp.maximum, tops)
        total = jnp.zeros((1, 2 * T), jnp.float32)
        delta = jnp.zeros((1, 2 * T), jnp.float32)
        for j in range(5):
            rows = pl.ds((b + j) * T, T)
            here = pl.ds(j * T, T)
            t = top
            if j < 4:
                t = jnp.where(first + b + j >= 0, top, -NEG)
            p = jnp.exp2((s_scr[here, :] - t) * (SCALE * LOG2E))
            g = dot(kv[i, 1, rows, :], dob)
            total = total + jnp.sum(p, axis=0, keepdims=True)
            delta = delta + jnp.sum(p * g, axis=0, keepdims=True)
            p_scr[here, :] = p
            g_scr[here, :] = g
        inv = 1.0 / total
        delta = delta * inv
        for j in range(5):
            rows = pl.ds((b + j) * T, T)
            here = pl.ds(j * T, T)
            p = p_scr[here, :] * inv
            ds = (p * (g_scr[here, :] - delta)).astype(jnp.bfloat16)
            ds_scr[here, :] = ds
            dv = dot(p.astype(jnp.bfloat16), dob, NT)
            dk = dot(ds, qb) * SCALE
            if b == 0 or j == 4:
                acc[i, 0, rows, :] = dk
                acc[i, 1, rows, :] = dv
            else:
                acc[i, 0, rows, :] += dk
                acc[i, 1, rows, :] += dv
        dqt = dot(kv[i, 0, pl.ds(b * T, 5 * T), :], ds_scr[...], TN)
        dq[b, pl.ds(2 * i, 2)] = (
            (jnp.transpose(dqt) * SCALE).astype(jnp.bfloat16).reshape(2, T, D)
        )


def kernel(
    n, q_in, k_in, v_in, do_in, dq_out, dkv_out,
    kv, q, do, dq, s_scr, p_scr, g_scr, ds_scr, acc,
    part_a, got_a, part_b, got_b, fin,
    loc_sem, d2d_send, d2d_recv, fb_send, fb_recv, fa_send, fa_recv,
    ra_send, ra_recv, rb_send, rb_recv, out_loc, out_send, out_recv, go_send, go_recv,
):
    me = lax.axis_index("ctx")
    core = lax.rem(me, 2)
    chip = me // 2
    sib = 2 * chip + (1 - core)
    nxt = lax.rem(me + 2, n)
    prv = lax.rem(me + n - 2, n)

    chips = n // 2
    worker = me // chips
    head = lax.rem(me // 4, 2 * HK)
    quarter = lax.rem(me, 4)
    stays = worker == core

    slab = pl.ds(pl.multiple_of(core * T, T), T)
    own = pl.ds(pl.multiple_of(4 * T + core * T, T), T)
    mine8 = pl.ds(HK * core, HK)
    theirs8 = pl.ds(HK * (1 - core), HK)
    mine16 = pl.ds(2 * HK * core, 2 * HK)
    theirs16 = pl.ds(2 * HK * (1 - core), 2 * HK)

    starts = [
        (k_in, mine8, theirs8, kv.at[:, 0, own]),
        (v_in, mine8, theirs8, kv.at[:, 1, own]),
        (q_in, mine16, theirs16, q.at[core]),
    ]
    local = []
    for at, (src, mine, _, dst) in enumerate(starts):
        local.append(pltpu.make_async_copy(src.at[mine], dst, loc_sem.at[at]))
        local[-1].start()

    barrier = pltpu.get_barrier_semaphore()
    for other in (sib, nxt, prv):
        pl.semaphore_signal(barrier, inc=1, device_id=(other,), device_id_type=MESH)

    def greet(i, carry):
        sender = chips * core + i

        @pl.when(sender != me)
        def _():
            pl.semaphore_signal(barrier, inc=1, device_id=(sender,), device_id_type=MESH)

        return carry

    lax.fori_loop(0, chips, greet, 0)
    pl.semaphore_wait(barrier, 3 + chips - jnp.where(stays, 1, 0))

    def remote(src, dst, send, recv, dev):
        return pltpu.make_async_remote_copy(
            src_ref=src, dst_ref=dst, send_sem=send, recv_sem=recv,
            device_id=(dev,), device_id_type=MESH,
        )

    cross = []
    for at, (src, _, theirs, dst) in enumerate(starts):
        cross.append(remote(src.at[theirs], dst, d2d_send.at[at], d2d_recv.at[at], sib))
        cross[-1].start()

    def piece(i):
        to = lax.rem(chip + 21 * i, chips)
        return (
            do_in.at[:, pl.ds(pl.multiple_of(to * 2 * T, 2 * T), 2 * T)],
            do.at[head, pl.ds(pl.multiple_of(quarter * 32, 32), 32), :],
            2 * to + worker,
        )

    def spread(i):
        src, dst, dev = piece(i)
        return remote(src, dst, go_send.at[i], go_recv.at[head], dev)

    def keep():
        src, dst, _ = piece(0)
        return pltpu.make_async_copy(src, dst, go_recv.at[head])

    def spread_start(i, carry):
        spread(i).start()
        return carry

    def to_b(i):
        return remote(
            kv.at[i, :, pl.ds(4 * T, 2 * T)], kv.at[i, :, pl.ds(2 * T, 2 * T)],
            fb_send.at[i], fb_recv.at[i], nxt,
        )

    def to_a(i):
        return remote(
            kv.at[i, :, pl.ds(2 * T, 2 * T)], kv.at[i, :, pl.ds(0, 2 * T)],
            fa_send.at[i], fa_recv.at[i], nxt,
        )

    def back_a(i):
        return remote(part_a.at[i], got_a.at[i], ra_send.at[i], ra_recv.at[i], prv)

    def back_b(i):
        return remote(part_b.at[i], got_b.at[i], rb_send.at[i], rb_recv.at[i], prv)

    def dq_copies(i):
        heads = pl.ds(2 * (HK * core + i), 2)
        return (
            pltpu.make_async_copy(dq.at[core, pl.ds(2 * i, 2)], dq_out.at[heads], out_loc.at[0, i]),
            remote(
                dq.at[1 - core, pl.ds(2 * i, 2)], dq_out.at[heads],
                out_send.at[0, i], out_recv.at[0, i], sib,
            ),
        )

    def dkv_copies(i):
        head = HK * core + i
        other = pl.ds(pl.multiple_of((1 - core) * T, T), T)
        return (
            pltpu.make_async_copy(fin.at[i, :, slab], dkv_out.at[head], out_loc.at[1, i]),
            remote(
                fin.at[i, :, other], dkv_out.at[head], out_send.at[1, i], out_recv.at[1, i], sib
            ),
        )

    @pl.when(stays)
    def _():
        keep().start()

    @pl.when(jnp.logical_not(stays))
    def _():
        spread(0).start()

    lax.fori_loop(1, chips, spread_start, 0)
    for at in (0, 1):
        local[at].wait()
        cross[at].wait_recv()
    for i in range(3):
        to_b(i).start()
    local[2].wait()
    cross[2].wait_recv()
    to_b(0).wait_recv()
    to_a(0).start()

    first = 2 * chip - 4

    def back1(i):
        back_a(i).wait_recv()
        part_b[i] = (acc[i, :, 2 * T : 4 * T, :] + got_a[i].astype(jnp.float32)).astype(jnp.bfloat16)
        back_b(i).start()

    def back2(i):
        back_b(i).wait_recv()
        fin[i] = (acc[i, :, 4 * T :, :] + got_b[i].astype(jnp.float32)).astype(jnp.bfloat16)
        for copy in dkv_copies(i):
            copy.start()

    def step(i, carry):
        @pl.when(i + 1 < HK)
        def _():
            to_b(i + 1).wait_recv()
            to_a(i + 1).start()

        @pl.when(i + 3 < HK)
        def _():
            to_b(i + 3).start()

        to_a(i).wait_recv()
        for h in range(2):
            pltpu.make_async_copy(do.at[2 * i + h], do.at[2 * i + h], go_recv.at[2 * i + h]).wait()
        attend(i, first, kv, q, do, s_scr, p_scr, g_scr, ds_scr, acc, dq)
        part_a[i] = acc[i, :, : 2 * T, :].astype(jnp.bfloat16)
        back_a(i).start()
        for copy in dq_copies(i):
            copy.start()

        @pl.when(i >= 1)
        def _():
            back1(i - 1)

        @pl.when(i >= 2)
        def _():
            back2(i - 2)

        return carry

    lax.fori_loop(0, HK, step, 0)
    back1(HK - 1)
    back2(HK - 2)
    back2(HK - 1)

    for copy in cross:
        copy.wait_send()

    def finish(i, carry):
        to_b(i).wait_send()
        to_a(i).wait_send()
        back_a(i).wait_send()
        back_b(i).wait_send()
        for here, there in (dq_copies(i), dkv_copies(i)):
            here.wait()
            there.wait()
        return carry

    lax.fori_loop(0, HK, finish, 0)

    @pl.when(jnp.logical_not(stays))
    def _():
        spread(0).wait_send()

    def spread_done(i, carry):
        spread(i).wait_send()
        return carry

    lax.fori_loop(1, chips, spread_done, 0)


def on_device(query_rows, key_rows, value_rows, grad_out):
    n = lax.axis_size("ctx")
    q_in = jnp.transpose(query_rows, (1, 0, 2))
    k_in = jnp.transpose(key_rows, (1, 0, 2))
    v_in = jnp.transpose(value_rows, (1, 0, 2))
    dma = pltpu.SemaphoreType.DMA
    bf16, f32 = jnp.bfloat16, jnp.float32
    any_spec = pl.BlockSpec(memory_space=pl.ANY)
    dq_heads, dkv = pl.pallas_call(
        functools.partial(kernel, n),
        out_shape=(
            jax.ShapeDtypeStruct((4 * HK, T, D), bf16),
            jax.ShapeDtypeStruct((2 * HK, 2, T, D), bf16),
        ),
        in_specs=[any_spec] * 4,
        out_specs=(any_spec, any_spec),
        scratch_shapes=[
            pltpu.VMEM((HK, 2, 6 * T, D), bf16),
            pltpu.VMEM((2, 2 * HK, T, D), bf16),
            pltpu.VMEM((2 * HK, D, 2 * T), bf16),
            pltpu.VMEM((2, 2 * HK, T, D), bf16),
            pltpu.VMEM((5 * T, 2 * T), f32),
            pltpu.VMEM((5 * T, 2 * T), f32),
            pltpu.VMEM((5 * T, 2 * T), f32),
            pltpu.VMEM((5 * T, 2 * T), bf16),
            pltpu.VMEM((HK, 2, 6 * T, D), f32),
            pltpu.VMEM((HK, 2, 2 * T, D), bf16),
            pltpu.VMEM((HK, 2, 2 * T, D), bf16),
            pltpu.VMEM((HK, 2, 2 * T, D), bf16),
            pltpu.VMEM((HK, 2, 2 * T, D), bf16),
            pltpu.VMEM((HK, 2, 2 * T, D), bf16),
            dma((3,)), dma((3,)), dma((3,)),
            dma((HK,)), dma((HK,)), dma((HK,)), dma((HK,)),
            dma((HK,)), dma((HK,)), dma((HK,)), dma((HK,)),
            dma((2, HK)), dma((2, HK)), dma((2, HK)),
            dma((n // 2,)), dma((2 * HK,)),
        ],
        compiler_params=pltpu.CompilerParams(
            collective_id=0, has_side_effects=True, vmem_limit_bytes=58 * 2**20
        ),
        cost_estimate=pl.CostEstimate(
            flops=14_000_000_000, bytes_accessed=12 * 2**20, transcendentals=10_000_000
        ),
    )(q_in, k_in, v_in, grad_out)
    grad_query = jnp.transpose(dq_heads, (1, 0, 2))
    grad_key = jnp.transpose(dkv[:, 0], (1, 0, 2))
    grad_value = jnp.transpose(dkv[:, 1], (1, 0, 2))
    return (grad_query, grad_key, grad_value)


def solution(mesh):
    in_specs = (P("ctx", None, None), P("ctx", None, None), P("ctx", None, None), P("ctx", None))
    out_specs = (P("ctx", None, None), P("ctx", None, None), P("ctx", None, None))
    return jax.shard_map(
        on_device, mesh=mesh, in_specs=in_specs, out_specs=out_specs, check_vma=False
    )
```

```python
import functools

import jax
import jax.numpy as jnp
from jax import lax
from jax.experimental import pallas as pl
from jax.experimental.pallas import tpu as pltpu
from jax.sharding import PartitionSpec as P

MESH = pl.DeviceIdType.MESH
SCALE = 1.0 / 12.0
LOG2E = 1.4426950408889634
T = 256
D = 128
HK = 8
NEG = -1e30

NT = (((1,), (1,)), ((), ()))
TN = (((0,), (0,)), ((), ()))


def dot(a, b, dims=(((1,), (0,)), ((), ()))):
    return lax.dot_general(a, b, dims, preferred_element_type=jnp.float32)


def attend(i, first, kv, q, do, s_scr, p_scr, g_scr, ds_scr, acc, dq):
    row = lax.broadcasted_iota(jnp.int32, (T, T), 0)
    col = lax.broadcasted_iota(jnp.int32, (T, T), 1)
    after = row > col
    after = jnp.concatenate([after, after], axis=1)
    for b in range(2):
        qb = q[b, pl.ds(2 * i, 2)].reshape(2 * T, D)
        dob = jnp.concatenate(
            [do[2 * i, :, b * T : (b + 1) * T], do[2 * i + 1, :, b * T : (b + 1) * T]], axis=1
        )
        tops = []
        for j in range(5):
            rows = pl.ds((b + j) * T, T)
            s = dot(kv[i, 0, rows, :], qb, NT)
            if j == 0:
                s = jnp.where(after, s, NEG)
            if j == 4:
                s = jnp.where(after, NEG, s)
            s_scr[pl.ds(j * T, T), :] = s
            t = jnp.max(s, axis=0, keepdims=True)
            if j < 4:
                t = jnp.where(first + b + j >= 0, t, NEG)
            tops.append(t)
        top = functools.reduce(jnp.maximum, tops)
        total = jnp.zeros((1, 2 * T), jnp.float32)
        delta = jnp.zeros((1, 2 * T), jnp.float32)
        for j in range(5):
            rows = pl.ds((b + j) * T, T)
            here = pl.ds(j * T, T)
            t = top
            if j < 4:
                t = jnp.where(first + b + j >= 0, top, -NEG)
            p = jnp.exp2((s_scr[here, :] - t) * (SCALE * LOG2E))
            g = dot(kv[i, 1, rows, :], dob)
            total = total + jnp.sum(p, axis=0, keepdims=True)
            delta = delta + jnp.sum(p * g, axis=0, keepdims=True)
            p_scr[here, :] = p
            g_scr[here, :] = g
        inv = 1.0 / total
        delta = delta * inv
        for j in range(5):
            rows = pl.ds((b + j) * T, T)
            here = pl.ds(j * T, T)
            p = p_scr[here, :] * inv
            ds = (p * (g_scr[here, :] - delta)).astype(jnp.bfloat16)
            ds_scr[here, :] = ds
            dv = dot(p.astype(jnp.bfloat16), dob, NT)
            dk = dot(ds, qb) * SCALE
            if b == 0 or j == 4:
                acc[i, 0, rows, :] = dk
                acc[i, 1, rows, :] = dv
            else:
                acc[i, 0, rows, :] += dk
                acc[i, 1, rows, :] += dv
        dqt = dot(kv[i, 0, pl.ds(b * T, 5 * T), :], ds_scr[...], TN)
        dq[b, pl.ds(2 * i, 2)] = (
            (jnp.transpose(dqt) * SCALE).astype(jnp.bfloat16).reshape(2, T, D)
        )


def kernel(
    n, q_in, k_in, v_in, do_in, dq_out, dkv_out,
    q_raw, k_raw, v_raw, q_heads, kv_heads,
    kv, q, do, dq, s_scr, p_scr, g_scr, ds_scr, acc,
    part_a, got_a, part_b, got_b, fin,
    loc_sem, d2d_send, d2d_recv, fb_send, fb_recv, fa_send, fa_recv,
    ra_send, ra_recv, rb_send, rb_recv, out_loc, out_send, out_recv, go_send, go_recv,
):
    me = lax.axis_index("ctx")
    core = lax.rem(me, 2)
    chip = me // 2
    sib = 2 * chip + (1 - core)
    nxt = lax.rem(me + 2, n)
    prv = lax.rem(me + n - 2, n)

    chips = n // 2
    worker = me // chips
    head = lax.rem(me // 4, 2 * HK)
    quarter = lax.rem(me, 4)
    stays = worker == core

    slab = pl.ds(pl.multiple_of(core * T, T), T)
    own = pl.ds(pl.multiple_of(4 * T + core * T, T), T)
    local = []
    for at, (src, dst) in enumerate(((k_in, k_raw), (v_in, v_raw), (q_in, q_raw))):
        local.append(pltpu.make_async_copy(src, dst, loc_sem.at[at]))
        local[-1].start()

    barrier = pltpu.get_barrier_semaphore()
    for other in (sib, nxt, prv):
        pl.semaphore_signal(barrier, inc=1, device_id=(other,), device_id_type=MESH)

    def greet(i, carry):
        sender = chips * core + i

        @pl.when(sender != me)
        def _():
            pl.semaphore_signal(barrier, inc=1, device_id=(sender,), device_id_type=MESH)

        return carry

    lax.fori_loop(0, chips, greet, 0)
    pl.semaphore_wait(barrier, 3 + chips - jnp.where(stays, 1, 0))

    def remote(src, dst, send, recv, dev):
        return pltpu.make_async_remote_copy(
            src_ref=src, dst_ref=dst, send_sem=send, recv_sem=recv,
            device_id=(dev,), device_id_type=MESH,
        )

    def piece(i):
        to = lax.rem(chip + 21 * i, chips)
        return (
            do_in.at[:, pl.ds(pl.multiple_of(to * 2 * T, 2 * T), 2 * T)],
            do.at[head, pl.ds(pl.multiple_of(quarter * 32, 32), 32), :],
            2 * to + worker,
        )

    def spread(i):
        src, dst, dev = piece(i)
        return remote(src, dst, go_send.at[i], go_recv.at[head], dev)

    def keep():
        src, dst, _ = piece(0)
        return pltpu.make_async_copy(src, dst, go_recv.at[head])

    def spread_start(i, carry):
        spread(i).start()
        return carry

    def to_b(i):
        return remote(
            kv.at[i, :, pl.ds(4 * T, 2 * T)], kv.at[i, :, pl.ds(2 * T, 2 * T)],
            fb_send.at[i], fb_recv.at[i], nxt,
        )

    def to_a(i):
        return remote(
            kv.at[i, :, pl.ds(2 * T, 2 * T)], kv.at[i, :, pl.ds(0, 2 * T)],
            fa_send.at[i], fa_recv.at[i], nxt,
        )

    def back_a(i):
        return remote(part_a.at[i], got_a.at[i], ra_send.at[i], ra_recv.at[i], prv)

    def back_b(i):
        return remote(part_b.at[i], got_b.at[i], rb_send.at[i], rb_recv.at[i], prv)

    def dq_copies(i):
        heads = pl.ds(2 * (HK * core + i), 2)
        return (
            pltpu.make_async_copy(dq.at[core, pl.ds(2 * i, 2)], dq_out.at[heads], out_loc.at[0, i]),
            remote(
                dq.at[1 - core, pl.ds(2 * i, 2)], dq_out.at[heads],
                out_send.at[0, i], out_recv.at[0, i], sib,
            ),
        )

    def dkv_copies(i):
        head = HK * core + i
        other = pl.ds(pl.multiple_of((1 - core) * T, T), T)
        return (
            pltpu.make_async_copy(fin.at[i, :, slab], dkv_out.at[head], out_loc.at[1, i]),
            remote(
                fin.at[i, :, other], dkv_out.at[head], out_send.at[1, i], out_recv.at[1, i], sib
            ),
        )

    @pl.when(stays)
    def _():
        keep().start()

    @pl.when(jnp.logical_not(stays))
    def _():
        spread(0).start()

    lax.fori_loop(1, chips, spread_start, 0)
    moves = [
        (kv_heads.at[core], kv_heads.at[1 - core], kv.at[:, :, own]),
        (q_heads.at[core], q_heads.at[1 - core], q.at[core]),
    ]
    cross, keeps = [], []
    for at, (mine, theirs, dst) in enumerate(moves):
        cross.append(remote(theirs, dst, d2d_send.at[at], d2d_recv.at[at], sib))
        keeps.append(pltpu.make_async_copy(mine, dst, loc_sem.at[3 + at]))

    def turn_kv(i, carry):
        rows = pl.ds(pl.multiple_of(i * 16, 16), 16)
        for at, raw in enumerate((k_raw, v_raw)):
            turned = jnp.swapaxes(raw[rows], 0, 1)
            for half in range(2):
                kv_heads[half, :, at, rows, :] = turned[half * HK : (half + 1) * HK]
        return carry

    def turn_q(i, carry):
        rows = pl.ds(pl.multiple_of(i * 16, 16), 16)
        turned = jnp.swapaxes(q_raw[rows], 0, 1)
        for half in range(2):
            q_heads[half, :, rows, :] = turned[half * 2 * HK : (half + 1) * 2 * HK]
        return carry

    local[0].wait()
    local[1].wait()
    lax.fori_loop(0, T // 16, turn_kv, 0)
    cross[0].start()
    keeps[0].start()
    keeps[0].wait()
    cross[0].wait_recv()
    for i in range(3):
        to_b(i).start()
    local[2].wait()
    lax.fori_loop(0, T // 16, turn_q, 0)
    cross[1].start()
    keeps[1].start()
    keeps[1].wait()
    cross[1].wait_recv()
    to_b(0).wait_recv()
    to_a(0).start()

    first = 2 * chip - 4

    def back1(i):
        back_a(i).wait_recv()
        part_b[i] = (acc[i, :, 2 * T : 4 * T, :] + got_a[i].astype(jnp.float32)).astype(jnp.bfloat16)
        back_b(i).start()

    def back2(i):
        back_b(i).wait_recv()
        fin[i] = (acc[i, :, 4 * T :, :] + got_b[i].astype(jnp.float32)).astype(jnp.bfloat16)
        for copy in dkv_copies(i):
            copy.start()

    def step(i, carry):
        @pl.when(i + 1 < HK)
        def _():
            to_b(i + 1).wait_recv()
            to_a(i + 1).start()

        @pl.when(i + 3 < HK)
        def _():
            to_b(i + 3).start()

        to_a(i).wait_recv()
        for h in range(2):
            pltpu.make_async_copy(do.at[2 * i + h], do.at[2 * i + h], go_recv.at[2 * i + h]).wait()
        attend(i, first, kv, q, do, s_scr, p_scr, g_scr, ds_scr, acc, dq)
        part_a[i] = acc[i, :, : 2 * T, :].astype(jnp.bfloat16)
        back_a(i).start()
        for copy in dq_copies(i):
            copy.start()

        @pl.when(i >= 1)
        def _():
            back1(i - 1)

        @pl.when(i >= 2)
        def _():
            back2(i - 2)

        return carry

    lax.fori_loop(0, HK, step, 0)
    back1(HK - 1)
    back2(HK - 2)
    back2(HK - 1)

    for copy in cross:
        copy.wait_send()

    def finish(i, carry):
        to_b(i).wait_send()
        to_a(i).wait_send()
        back_a(i).wait_send()
        back_b(i).wait_send()
        for here, there in (dq_copies(i), dkv_copies(i)):
            here.wait()
            there.wait()
        return carry

    lax.fori_loop(0, HK, finish, 0)

    @pl.when(jnp.logical_not(stays))
    def _():
        spread(0).wait_send()

    def spread_done(i, carry):
        spread(i).wait_send()
        return carry

    lax.fori_loop(1, chips, spread_done, 0)


def turn_back(dq_ref, dkv_ref, gq_ref, gk_ref, gv_ref):
    for r in range(0, dq_ref.shape[1], 16):
        rows = pl.ds(r, 16)
        gq_ref[rows] = jnp.swapaxes(dq_ref[:, rows, :], 0, 1)
        gk_ref[rows] = jnp.swapaxes(dkv_ref[:, 0, rows, :], 0, 1)
        gv_ref[rows] = jnp.swapaxes(dkv_ref[:, 1, rows, :], 0, 1)


def on_device(query_rows, key_rows, value_rows, grad_out):
    n = lax.axis_size("ctx")
    dma = pltpu.SemaphoreType.DMA
    bf16, f32 = jnp.bfloat16, jnp.float32
    any_spec = pl.BlockSpec(memory_space=pl.ANY)
    dq_heads, dkv = pl.pallas_call(
        functools.partial(kernel, n),
        out_shape=(
            jax.ShapeDtypeStruct((4 * HK, T, D), bf16),
            jax.ShapeDtypeStruct((2 * HK, 2, T, D), bf16),
        ),
        in_specs=[any_spec] * 4,
        out_specs=(any_spec, any_spec),
        scratch_shapes=[
            pltpu.VMEM((T, 4 * HK, D), bf16),
            pltpu.VMEM((T, 2 * HK, D), bf16),
            pltpu.VMEM((T, 2 * HK, D), bf16),
            pltpu.VMEM((2, 2 * HK, T, D), bf16),
            pltpu.VMEM((2, HK, 2, T, D), bf16),
            pltpu.VMEM((HK, 2, 6 * T, D), bf16),
            pltpu.VMEM((2, 2 * HK, T, D), bf16),
            pltpu.VMEM((2 * HK, D, 2 * T), bf16),
            pltpu.VMEM((2, 2 * HK, T, D), bf16),
            pltpu.VMEM((5 * T, 2 * T), f32),
            pltpu.VMEM((5 * T, 2 * T), f32),
            pltpu.VMEM((5 * T, 2 * T), f32),
            pltpu.VMEM((5 * T, 2 * T), bf16),
            pltpu.VMEM((HK, 2, 6 * T, D), f32),
            pltpu.VMEM((HK, 2, 2 * T, D), bf16),
            pltpu.VMEM((HK, 2, 2 * T, D), bf16),
            pltpu.VMEM((HK, 2, 2 * T, D), bf16),
            pltpu.VMEM((HK, 2, 2 * T, D), bf16),
            pltpu.VMEM((HK, 2, 2 * T, D), bf16),
            dma((5,)), dma((2,)), dma((2,)),
            dma((HK,)), dma((HK,)), dma((HK,)), dma((HK,)),
            dma((HK,)), dma((HK,)), dma((HK,)), dma((HK,)),
            dma((2, HK)), dma((2, HK)), dma((2, HK)),
            dma((n // 2,)), dma((2 * HK,)),
        ],
        compiler_params=pltpu.CompilerParams(
            collective_id=0, has_side_effects=True, vmem_limit_bytes=58 * 2**20
        ),
        cost_estimate=pl.CostEstimate(
            flops=14_000_000_000, bytes_accessed=12 * 2**20, transcendentals=10_000_000
        ),
    )(query_rows, key_rows, value_rows, grad_out)
    rows = 64
    return pl.pallas_call(
        turn_back,
        grid=(T // rows,),
        out_shape=(
            jax.ShapeDtypeStruct(query_rows.shape, bf16),
            jax.ShapeDtypeStruct(key_rows.shape, bf16),
            jax.ShapeDtypeStruct(value_rows.shape, bf16),
        ),
        in_specs=[
            pl.BlockSpec((4 * HK, rows, D), lambda i: (0, i, 0)),
            pl.BlockSpec((2 * HK, 2, rows, D), lambda i: (0, 0, i, 0)),
        ],
        out_specs=(
            pl.BlockSpec((rows, 4 * HK, D), lambda i: (i, 0, 0)),
            pl.BlockSpec((rows, 2 * HK, D), lambda i: (i, 0, 0)),
            pl.BlockSpec((rows, 2 * HK, D), lambda i: (i, 0, 0)),
        ),
    )(dq_heads, dkv)


def solution(mesh):
    in_specs = (P("ctx", None, None), P("ctx", None, None), P("ctx", None, None), P("ctx", None))
    out_specs = (P("ctx", None, None), P("ctx", None, None), P("ctx", None, None))
    return jax.shard_map(
        on_device, mesh=mesh, in_specs=in_specs, out_specs=out_specs, check_vma=False
    )
```

```python
import functools

import jax
import jax.numpy as jnp
from jax import lax
from jax.experimental import pallas as pl
from jax.experimental.pallas import tpu as pltpu
from jax.sharding import PartitionSpec as P

MESH = pl.DeviceIdType.MESH
SCALE = 1.0 / 12.0
LOG2E = 1.4426950408889634
T = 256
D = 128
HK = 8
NEG = -1e30

NT = (((1,), (1,)), ((), ()))
TN = (((0,), (0,)), ((), ()))


def dot(a, b, dims=(((1,), (0,)), ((), ()))):
    return lax.dot_general(a, b, dims, preferred_element_type=jnp.float32)


def attend(i, first, kv, q, do, s_scr, p_scr, g_scr, ds_scr, acc, dq):
    row = lax.broadcasted_iota(jnp.int32, (T, T), 0)
    col = lax.broadcasted_iota(jnp.int32, (T, T), 1)
    after = row > col
    after = jnp.concatenate([after, after], axis=1)
    for b in range(2):
        qb = q[b, pl.ds(2 * i, 2)].reshape(2 * T, D)
        dob = jnp.concatenate(
            [do[2 * i, :, b * T : (b + 1) * T], do[2 * i + 1, :, b * T : (b + 1) * T]], axis=1
        )
        tops = []
        for j in range(5):
            rows = pl.ds((b + j) * T, T)
            s = dot(kv[i, 0, rows, :], qb, NT)
            if j == 0:
                s = jnp.where(after, s, NEG)
            if j == 4:
                s = jnp.where(after, NEG, s)
            s_scr[pl.ds(j * T, T), :] = s
            t = jnp.max(s, axis=0, keepdims=True)
            if j < 4:
                t = jnp.where(first + b + j >= 0, t, NEG)
            tops.append(t)
        top = functools.reduce(jnp.maximum, tops)
        total = jnp.zeros((1, 2 * T), jnp.float32)
        delta = jnp.zeros((1, 2 * T), jnp.float32)
        for j in range(5):
            rows = pl.ds((b + j) * T, T)
            here = pl.ds(j * T, T)
            t = top
            if j < 4:
                t = jnp.where(first + b + j >= 0, top, -NEG)
            p = jnp.exp2((s_scr[here, :] - t) * (SCALE * LOG2E))
            g = dot(kv[i, 1, rows, :], dob)
            total = total + jnp.sum(p, axis=0, keepdims=True)
            delta = delta + jnp.sum(p * g, axis=0, keepdims=True)
            p_scr[here, :] = p
            g_scr[here, :] = g
        inv = 1.0 / total
        delta = delta * inv
        for j in range(5):
            rows = pl.ds((b + j) * T, T)
            here = pl.ds(j * T, T)
            p = p_scr[here, :] * inv
            ds = (p * (g_scr[here, :] - delta)).astype(jnp.bfloat16)
            ds_scr[here, :] = ds
            dv = dot(p.astype(jnp.bfloat16), dob, NT)
            dk = dot(ds, qb) * SCALE
            if b == 0 or j == 4:
                acc[i, 0, rows, :] = dk
                acc[i, 1, rows, :] = dv
            else:
                acc[i, 0, rows, :] += dk
                acc[i, 1, rows, :] += dv
        dqt = dot(kv[i, 0, pl.ds(b * T, 5 * T), :], ds_scr[...], TN)
        dq[b, pl.ds(2 * i, 2)] = (
            (jnp.transpose(dqt) * SCALE).astype(jnp.bfloat16).reshape(2, T, D)
        )


def kernel(
    n, q_in, k_in, v_in, do_in, dq_out, dkv_out,
    q_raw, k_raw, v_raw, q_heads, kv_heads,
    kv, q, do, dq, s_scr, p_scr, g_scr, ds_scr, acc,
    part_a, got_a, part_b, got_b, fin,
    loc_sem, d2d_send, d2d_recv, fb_send, fb_recv, fa_send, fa_recv,
    ra_send, ra_recv, rb_send, rb_recv, out_loc, out_send, out_recv, go_send, go_recv,
):
    me = lax.axis_index("ctx")
    core = lax.rem(me, 2)
    chip = me // 2
    sib = 2 * chip + (1 - core)
    nxt = lax.rem(me + 2, n)
    prv = lax.rem(me + n - 2, n)

    chips = n // 2
    worker = me // chips
    head = lax.rem(me // 4, 2 * HK)
    quarter = lax.rem(me, 4)
    stays = worker == core

    slab = pl.ds(pl.multiple_of(core * T, T), T)
    own = pl.ds(pl.multiple_of(4 * T + core * T, T), T)
    local = []
    for at, (src, dst) in enumerate(((k_in, k_raw), (v_in, v_raw), (q_in, q_raw))):
        local.append(pltpu.make_async_copy(src, dst, loc_sem.at[at]))
        local[-1].start()

    barrier = pltpu.get_barrier_semaphore()
    for other in (sib, nxt, prv):
        pl.semaphore_signal(barrier, inc=1, device_id=(other,), device_id_type=MESH)

    def greet(i, carry):
        sender = chips * core + i

        @pl.when(sender != me)
        def _():
            pl.semaphore_signal(barrier, inc=1, device_id=(sender,), device_id_type=MESH)

        return carry

    lax.fori_loop(0, chips, greet, 0)
    pl.semaphore_wait(barrier, 3 + chips - jnp.where(stays, 1, 0))

    def remote(src, dst, send, recv, dev):
        return pltpu.make_async_remote_copy(
            src_ref=src, dst_ref=dst, send_sem=send, recv_sem=recv,
            device_id=(dev,), device_id_type=MESH,
        )

    def piece(i):
        to = lax.rem(chip + 21 * i, chips)
        return (
            do_in.at[:, pl.ds(pl.multiple_of(to * 2 * T, 2 * T), 2 * T)],
            do.at[head, pl.ds(pl.multiple_of(quarter * 32, 32), 32), :],
            2 * to + worker,
        )

    def spread(i):
        src, dst, dev = piece(i)
        return remote(src, dst, go_send.at[i], go_recv.at[head], dev)

    def keep():
        src, dst, _ = piece(0)
        return pltpu.make_async_copy(src, dst, go_recv.at[head])

    def spread_start(i, carry):
        spread(i).start()
        return carry

    def to_b(i):
        return remote(
            kv.at[i, :, pl.ds(4 * T, 2 * T)], kv.at[i, :, pl.ds(2 * T, 2 * T)],
            fb_send.at[i], fb_recv.at[i], nxt,
        )

    def to_a(i):
        return remote(
            kv.at[i, :, pl.ds(2 * T, 2 * T)], kv.at[i, :, pl.ds(0, 2 * T)],
            fa_send.at[i], fa_recv.at[i], nxt,
        )

    def back_a(i):
        return remote(part_a.at[i], got_a.at[i], ra_send.at[i], ra_recv.at[i], prv)

    def back_b(i):
        return remote(part_b.at[i], got_b.at[i], rb_send.at[i], rb_recv.at[i], prv)

    def dq_copies(i):
        heads = pl.ds(2 * (HK * core + i), 2)
        return (
            pltpu.make_async_copy(dq.at[core, pl.ds(2 * i, 2)], dq_out.at[heads], out_loc.at[0, i]),
            remote(
                dq.at[1 - core, pl.ds(2 * i, 2)], dq_out.at[heads],
                out_send.at[0, i], out_recv.at[0, i], sib,
            ),
        )

    def dkv_copies(i):
        head = HK * core + i
        other = pl.ds(pl.multiple_of((1 - core) * T, T), T)
        return (
            pltpu.make_async_copy(fin.at[i, :, slab], dkv_out.at[head], out_loc.at[1, i]),
            remote(
                fin.at[i, :, other], dkv_out.at[head], out_send.at[1, i], out_recv.at[1, i], sib
            ),
        )

    @pl.when(stays)
    def _():
        keep().start()

    @pl.when(jnp.logical_not(stays))
    def _():
        spread(0).start()

    lax.fori_loop(1, chips, spread_start, 0)
    moves = [
        (kv_heads.at[core], kv_heads.at[1 - core], kv.at[:, :, own]),
        (q_heads.at[core], q_heads.at[1 - core], q.at[core]),
    ]
    cross, keeps = [], []
    for at, (mine, theirs, dst) in enumerate(moves):
        cross.append(remote(theirs, dst, d2d_send.at[at], d2d_recv.at[at], sib))
        keeps.append(pltpu.make_async_copy(mine, dst, loc_sem.at[3 + at]))

    def turn_kv(i, carry):
        rows = pl.ds(pl.multiple_of(i * 16, 16), 16)
        for at, raw in enumerate((k_raw, v_raw)):
            turned = jnp.swapaxes(raw[rows], 0, 1)
            for half in range(2):
                kv_heads[half, :, at, rows, :] = turned[half * HK : (half + 1) * HK]
        return carry

    def turn_q(i, carry):
        rows = pl.ds(pl.multiple_of(i * 16, 16), 16)
        turned = jnp.swapaxes(q_raw[rows], 0, 1)
        for half in range(2):
            q_heads[half, :, rows, :] = turned[half * 2 * HK : (half + 1) * 2 * HK]
        return carry

    local[0].wait()
    local[1].wait()
    lax.fori_loop(0, T // 16, turn_kv, 0)
    cross[0].start()
    keeps[0].start()
    keeps[0].wait()
    cross[0].wait_recv()
    for i in range(3):
        to_b(i).start()
    local[2].wait()
    lax.fori_loop(0, T // 16, turn_q, 0)
    cross[1].start()
    keeps[1].start()
    keeps[1].wait()
    cross[1].wait_recv()
    to_b(0).wait_recv()
    to_a(0).start()

    first = 2 * chip - 4

    def back1(i):
        back_a(i).wait_recv()
        part_b[i] = (acc[i, :, 2 * T : 4 * T, :] + got_a[i].astype(jnp.float32)).astype(jnp.bfloat16)
        back_b(i).start()

    def back2(i):
        back_b(i).wait_recv()
        fin[i] = (acc[i, :, 4 * T :, :] + got_b[i].astype(jnp.float32)).astype(jnp.bfloat16)
        for copy in dkv_copies(i):
            copy.start()

    def step(i, carry):
        @pl.when(i + 1 < HK)
        def _():
            to_b(i + 1).wait_recv()
            to_a(i + 1).start()

        @pl.when(i + 3 < HK)
        def _():
            to_b(i + 3).start()

        to_a(i).wait_recv()
        for h in range(2):
            pltpu.make_async_copy(do.at[2 * i + h], do.at[2 * i + h], go_recv.at[2 * i + h]).wait()
        attend(i, first, kv, q, do, s_scr, p_scr, g_scr, ds_scr, acc, dq)
        part_a[i] = acc[i, :, : 2 * T, :].astype(jnp.bfloat16)
        back_a(i).start()
        for copy in dq_copies(i):
            copy.start()

        @pl.when(i >= 1)
        def _():
            back1(i - 1)

        @pl.when(i >= 2)
        def _():
            back2(i - 2)

        return carry

    lax.fori_loop(0, HK, step, 0)
    back1(HK - 1)
    back2(HK - 2)
    back2(HK - 1)

    for copy in cross:
        copy.wait_send()

    def finish(i, carry):
        to_b(i).wait_send()
        to_a(i).wait_send()
        back_a(i).wait_send()
        back_b(i).wait_send()
        for here, there in (dq_copies(i), dkv_copies(i)):
            here.wait()
            there.wait()
        return carry

    lax.fori_loop(0, HK, finish, 0)

    @pl.when(jnp.logical_not(stays))
    def _():
        spread(0).wait_send()

    def spread_done(i, carry):
        spread(i).wait_send()
        return carry

    lax.fori_loop(1, chips, spread_done, 0)


def turn_back(dq_ref, dkv_ref, gq_ref, gk_ref, gv_ref):
    for r in range(0, dq_ref.shape[1], 16):
        rows = pl.ds(r, 16)
        gq_ref[rows] = jnp.swapaxes(dq_ref[:, rows, :], 0, 1)
        gk_ref[rows] = jnp.swapaxes(dkv_ref[:, 0, rows, :], 0, 1)
        gv_ref[rows] = jnp.swapaxes(dkv_ref[:, 1, rows, :], 0, 1)


def on_device(query_rows, key_rows, value_rows, grad_out):
    n = lax.axis_size("ctx")
    dma = pltpu.SemaphoreType.DMA
    bf16, f32 = jnp.bfloat16, jnp.float32
    any_spec = pl.BlockSpec(memory_space=pl.ANY)
    dq_heads, dkv = pl.pallas_call(
        functools.partial(kernel, n),
        out_shape=(
            jax.ShapeDtypeStruct((4 * HK, T, D), bf16),
            jax.ShapeDtypeStruct((2 * HK, 2, T, D), bf16),
        ),
        in_specs=[any_spec] * 4,
        out_specs=(any_spec, any_spec),
        scratch_shapes=[
            pltpu.VMEM((T, 4 * HK, D), bf16),
            pltpu.VMEM((T, 2 * HK, D), bf16),
            pltpu.VMEM((T, 2 * HK, D), bf16),
            pltpu.VMEM((2, 2 * HK, T, D), bf16),
            pltpu.VMEM((2, HK, 2, T, D), bf16),
            pltpu.VMEM((HK, 2, 6 * T, D), bf16),
            pltpu.VMEM((2, 2 * HK, T, D), bf16),
            pltpu.VMEM((2 * HK, D, 2 * T), bf16),
            pltpu.VMEM((2, 2 * HK, T, D), bf16),
            pltpu.VMEM((5 * T, 2 * T), f32),
            pltpu.VMEM((5 * T, 2 * T), f32),
            pltpu.VMEM((5 * T, 2 * T), f32),
            pltpu.VMEM((5 * T, 2 * T), bf16),
            pltpu.VMEM((HK, 2, 6 * T, D), f32),
            pltpu.VMEM((HK, 2, 2 * T, D), bf16),
            pltpu.VMEM((HK, 2, 2 * T, D), bf16),
            pltpu.VMEM((HK, 2, 2 * T, D), bf16),
            pltpu.VMEM((HK, 2, 2 * T, D), bf16),
            pltpu.VMEM((HK, 2, 2 * T, D), bf16),
            dma((5,)), dma((2,)), dma((2,)),
            dma((HK,)), dma((HK,)), dma((HK,)), dma((HK,)),
            dma((HK,)), dma((HK,)), dma((HK,)), dma((HK,)),
            dma((2, HK)), dma((2, HK)), dma((2, HK)),
            dma((n // 2,)), dma((2 * HK,)),
        ],
        compiler_params=pltpu.CompilerParams(
            collective_id=0, has_side_effects=True, vmem_limit_bytes=58 * 2**20
        ),
        cost_estimate=pl.CostEstimate(
            flops=14_000_000_000, bytes_accessed=12 * 2**20, transcendentals=10_000_000
        ),
    )(query_rows, key_rows, value_rows, grad_out)
    rows = 128
    return pl.pallas_call(
        turn_back,
        grid=(T // rows,),
        out_shape=(
            jax.ShapeDtypeStruct(query_rows.shape, bf16),
            jax.ShapeDtypeStruct(key_rows.shape, bf16),
            jax.ShapeDtypeStruct(value_rows.shape, bf16),
        ),
        in_specs=[
            pl.BlockSpec((4 * HK, rows, D), lambda i: (0, i, 0)),
            pl.BlockSpec((2 * HK, 2, rows, D), lambda i: (0, 0, i, 0)),
        ],
        out_specs=(
            pl.BlockSpec((rows, 4 * HK, D), lambda i: (i, 0, 0)),
            pl.BlockSpec((rows, 2 * HK, D), lambda i: (i, 0, 0)),
            pl.BlockSpec((rows, 2 * HK, D), lambda i: (i, 0, 0)),
        ),
    )(dq_heads, dkv)


def solution(mesh):
    in_specs = (P("ctx", None, None), P("ctx", None, None), P("ctx", None, None), P("ctx", None))
    out_specs = (P("ctx", None, None), P("ctx", None, None), P("ctx", None, None))
    return jax.shard_map(
        on_device, mesh=mesh, in_specs=in_specs, out_specs=out_specs, check_vma=False
    )
```
